256 devices in a mesh: grp: 32 (over z_hi, x, core), sp: 8 (over y, z_lo).
Axes of the slice: x: 4, y: 4, z: 8 (z_hi: 4, z_lo: 2; z = z_hi * 2 + z_lo), core: 2. Of those that a mesh axis runs over, the one named last changes fastest.
Arguments:
- queries: bfloat16 [32, 2048, 4096], P('grp', 'sp'), may hold values from -22 to 22
- keys: bfloat16 [32, 2048, 1024], P('grp', 'sp'), may hold values from -16 to 16
- values: bfloat16 [32, 2048, 1024], P('grp', 'sp'), may hold values from -6 to 6
- page_owner: int32 [32, 128, 1], P('grp'), may hold values from 0 to 31; in each aligned block of 128 rows (0 to 127, 128 to 255, ..., all dimensions but the last counted through in order) at most 8 rows name the same one
Outputs:
- attention: bfloat16 [32, 2048, 4096], P('grp', 'sp')
- key_cache: bfloat16 [8192, 16, 1024], P('grp', None, 'sp')
- value_cache: bfloat16 [8192, 16, 1024], P('grp', None, 'sp')
The draws below stay inside these ranges and needn't reach their ends.
Inputs may be any that keep to these rules, and one draw needn't show every extreme that they name: `page_owner`: for each prompt, no decode instance stores more than 8 of its pages, and in every draw some instance stores exactly 8 pages of some prompt.
All inputs are finite; a program needn't handle non-finite values.
Results may differ from the reference program's by a relative error of at most 0.0047.
Values may be sent and summed in bfloat16 or wider, within the bound.
No kernel may reach another device: no remote copies, remote signals or barrier semaphores. Data moves between devices by JAX's collectives and lax.ppermute only.
A program may use at most 128 MiB of HBM per device.

```python
import math
import jax
import jax.numpy as jnp
import numpy as np
from jax import lax

Q_HEADS = 32
KV_HEADS = 8
HEAD_DIM = 128
PROMPT_LEN = 2048
PAGE = 16
MOST = 8
PAGES = 128
GROUPS = 32


def draw_queries(key, part):
    key = jax.random.fold_in(key, 1)
    shape = (GROUPS, PROMPT_LEN, Q_HEADS, HEAD_DIM)
    base = jnp.clip(jax.random.normal(key, shape, jnp.float32), -6.0, 6.0)
    return base.reshape(GROUPS, PROMPT_LEN, Q_HEADS * HEAD_DIM).astype(jnp.bfloat16)


def draw_keys(key, part):
    key = jax.random.fold_in(key, 2)
    shape = (GROUPS, PROMPT_LEN, KV_HEADS, HEAD_DIM)
    base = jnp.clip(jax.random.normal(key, shape, jnp.float32), -6.0, 6.0)
    return base.reshape(GROUPS, PROMPT_LEN, KV_HEADS * HEAD_DIM).astype(jnp.bfloat16)


def shard_levels(rng, shape, pieces, least, largest):
    def one(dim, parts):
        draws = jax.random.uniform(jax.random.fold_in(jax.random.fold_in(rng, 6), dim), (parts,), jnp.float32, least / len(pieces), largest / len(pieces))
        return jnp.repeat(jnp.exp(draws), shape[dim] // parts).reshape((-1,) + (1,) * (len(shape) - dim - 1))

    gain = one(*pieces[0])
    for cut in pieces[1:]:
        gain = gain * one(*cut)
    return gain


def routed_block(key, own, number, rows, amount, top, bound, slope):
    sequence = jax.random.permutation(key, amount)
    crowded, ordinary = shares(amount, rows * top, bound, slope, True), shares(amount, rows * top, bound, slope, False)
    places = jnp.arange(amount)

    def named(tallies, offset_by):
        used = int((tallies > 0).sum())
        fixed = max(1, used // 4)
        moved = fixed + (places - fixed + offset_by * (used - fixed)) % max(1, amount - fixed)
        return jnp.zeros((amount,), jnp.int32).at[sequence[jnp.where(places < fixed, places, moved)]].set(jnp.asarray(tallies, jnp.int32))

    tallies = jnp.where(number % 4 == 0, named(crowded, number // 4), named(ordinary, number - number // 4 - 1))
    mixed = jax.random.permutation(jax.random.fold_in(own, 3), amount)
    source_of, receiver = mixed[0:amount // 2 * 2:2], mixed[1:amount // 2 * 2:2]
    room = jnp.minimum(tallies[source_of] - 1, bound - tallies[receiver]) // 2
    room = jnp.where((source_of == sequence[0]) | (receiver == sequence[0]) | (tallies[receiver] == 0), 0, jnp.maximum(room, 0))
    moved = jax.random.randint(jax.random.fold_in(own, 4), (amount // 2,), 0, 1 << 20) % (room + 1)
    tallies = tallies.at[source_of].add(-moved).at[receiver].add(moved)
    labels = jnp.searchsorted(jnp.cumsum(tallies), jnp.arange(rows * top), side="right").astype(jnp.int32)
    grid = labels.reshape(top, rows).T
    grid = grid[jax.random.permutation(jax.random.fold_in(own, 1), rows)]
    offset_by = jax.random.randint(jax.random.fold_in(own, 2), (rows, 1), 0, top)
    return jnp.take_along_axis(grid, (jnp.arange(top)[None, :] + offset_by) % top, axis=1)


def shares(number_of, total, most, slope, full):
    weights = [(1 << 20) // math.isqrt(grade ** slope) + 1 for grade in range(1, number_of + 1)]
    largest = most if full else min(most, max(-(-total // number_of), total * weights[0] // sum(weights)))
    least = 1 if total - largest >= number_of - 1 else 0
    holding, surplus = [largest] + [least] * (number_of - 1), total - largest - least * (number_of - 1)
    while surplus > 0:
        movable = [i for i in range(1, number_of) if holding[i] < largest] or [i for i in range(1, number_of) if holding[i] < most]
        mass, left = sum([weights[i] for i in movable]), surplus
        for i in movable:
            addition = min(most - holding[i], max(1, left * weights[i] // mass), surplus)
            holding[i] = holding[i] + addition
            surplus = surplus - addition
    return np.array(holding)


def centred(key, extent, scale, bound, pieces=(), held_as=jnp.bfloat16):
    entries = jax.random.normal(key, extent, jnp.float32) * scale
    if len(pieces) > 0:
        entries = shard_levels(key, extent, pieces, -0.22, 0.18) * entries
    return jnp.clip(entries, min=-bound, max=bound).astype(held_as)


def setup_inputs(seed: int = 0) -> dict:
    seeds = jax.random.split(jax.random.key(seed), 5)
    queries = draw_queries(jax.random.fold_in(seeds[4], 71), 0)
    keys = draw_keys(jax.random.fold_in(seeds[4], 71), 0)
    values = centred(seeds[2], (GROUPS, PROMPT_LEN, KV_HEADS * HEAD_DIM), 1.0, 6.0, ((0, 32), (1, 8)))
    page_owner_keys = jax.random.split(jax.random.fold_in(seeds[3], 1), GROUPS * PAGES // PAGES)
    page_owner_turns = jax.random.permutation(jax.random.fold_in(seeds[3], 3), GROUPS * PAGES // PAGES)
    page_owner = jax.vmap(lambda own, number: routed_block(jax.random.fold_in(seeds[3], 2), own, number, PAGES, GROUPS, 1, MOST, 2))(page_owner_keys, page_owner_turns).reshape((GROUPS, PAGES, 1))
    return dict(queries=queries, keys=keys, values=values, page_owner=page_owner)


def attend(queries, keys, values, first_pos, group):
    q_rows = queries.shape[0]
    k_rows = keys.shape[0]
    q_heads = queries.shape[1] // HEAD_DIM
    by_head = queries.reshape(q_rows, q_heads, HEAD_DIM).transpose(1, 0, 2)
    key_heads = keys.reshape(k_rows, -1, HEAD_DIM).transpose(1, 0, 2)
    value_heads = values.reshape(k_rows, -1, HEAD_DIM).transpose(1, 0, 2)
    allowed = jnp.arange(k_rows)[None, :] <= first_pos + jnp.arange(q_rows)[:, None]
    scale = HEAD_DIM ** -0.5

    def one_head(packed):
        query_head, source = packed
        key_head = lax.dynamic_index_in_dim(key_heads, source, 0, keepdims=False)
        value_head = lax.dynamic_index_in_dim(value_heads, source, 0, keepdims=False)
        scores = jnp.dot(query_head, key_head.T, preferred_element_type=jnp.float32) * scale
        scores = jnp.where(allowed, scores, -jnp.inf)
        shifted = jnp.exp(scores - jnp.max(scores, axis=1, keepdims=True))
        weights = (shifted / jnp.sum(shifted, axis=1, keepdims=True)).astype(jnp.bfloat16)
        return jnp.dot(weights, value_head, preferred_element_type=jnp.float32).astype(jnp.bfloat16)

    sources = (jnp.arange(q_heads) // group).astype(jnp.int32)
    result = lax.map(one_head, (by_head, sources))
    return result.transpose(1, 0, 2).reshape(q_rows, q_heads * HEAD_DIM)


def reference(queries, keys, values, page_owner):
    group = Q_HEADS // KV_HEADS
    attention = lax.map(lambda packed: attend(packed[0], packed[1], packed[2], 0, group), (queries, keys, values))
    count = GROUPS
    pages_n = PROMPT_LEN // PAGE
    owners = page_owner[:, :, 0]
    onehot = (owners[:, :, None] == jnp.arange(count)[None, None, :]).astype(jnp.int32)
    rank = jnp.sum(onehot * (jnp.cumsum(onehot, axis=1) - 1), axis=2)
    prompt_ids = jnp.arange(count)[:, None]
    target = ((owners * count + prompt_ids) * MOST + rank).reshape(-1)
    width = KV_HEADS * HEAD_DIM
    key_pages = keys.reshape(count * pages_n, PAGE, width)
    value_pages = values.reshape(count * pages_n, PAGE, width)
    empty = jnp.zeros((count * count * MOST, PAGE, width), jnp.bfloat16)
    key_cache = empty.at[target].set(key_pages)
    value_cache = empty.at[target].set(value_pages)
    return attention, key_cache, value_cache
```

```python
import functools

import jax
import jax.numpy as jnp
from jax import lax
from jax.experimental import pallas as pl
from jax.experimental.pallas import tpu as pltpu
from jax.sharding import Mesh, PartitionSpec as P

Q_HEADS = 32
KV_HEADS = 8
HEAD_DIM = 128
GROUP = Q_HEADS // KV_HEADS
SPAN = GROUP * HEAD_DIM
PAIR = 2 * HEAD_DIM
PAGE = 16
MOST = 8
LOG2E = 1.4426950408889634
SCALE2 = HEAD_DIM**-0.5 * LOG2E
GRP = ("zh", "x", "core")
SP = ("y", "zl")
YS = 4
ZS = 2


def call(kernel, outs, ins, copies=1, scratch=(), space=pltpu.VMEM, out_space=None, vmem=12, name=None, flops=0, moved=0, exps=0):
    out_space = out_space or space
    return pl.pallas_call(
        kernel,
        out_shape=outs,
        in_specs=[pl.BlockSpec(memory_space=pltpu.SMEM if x.dtype == jnp.int32 else space) for x in ins],
        out_specs=jax.tree.map(lambda _: pl.BlockSpec(memory_space=out_space), outs),
        scratch_shapes=[*scratch, *([pltpu.SemaphoreType.DMA((copies,))] if out_space == pl.ANY else [])],
        compiler_params=pltpu.CompilerParams(vmem_limit_bytes=vmem * 2**20),
        cost_estimate=pl.CostEstimate(flops=flops, bytes_accessed=moved, transcendentals=exps),
        name=name,
    )(*ins)


def move(pairs, sem, first=0):
    copies = [pltpu.make_async_copy(src, dst, sem.at[first + i]) for i, (src, dst) in enumerate(pairs)]
    for copy in copies:
        copy.start()
    for copy in copies:
        copy.wait()


def columns(ref, start, width):
    return ref.at[:, pl.ds(pl.multiple_of(start, width), width)]


def pair_of(k_ref, v_ref, head):
    return jnp.concatenate([columns(r, head * HEAD_DIM, HEAD_DIM)[...] for r in (k_ref, v_ref)], axis=1)


def kv_send_kernel(k_ref, v_ref, o_ref, k, v, out, sem):
    move([(k_ref, k), (v_ref, v)], sem)
    for h in range(KV_HEADS):
        out[h] = pair_of(k, v, h)
    move([(out, o_ref)], sem, 2)


def q_send_kernel(where_ref, q_ref, k_ref, v_ref, *o_refs):
    y, z = where_ref[0], where_ref[1]
    for d in range(YS):
        head = lax.rem(y + d, YS) * ZS + z
        o_refs[d][...] = columns(q_ref, head * SPAN, SPAN)[...]
    for d in range(YS):
        head = lax.rem(y + d, YS) * ZS + 1 - z
        o_refs[YS + d][:, :SPAN] = columns(q_ref, head * SPAN, SPAN)[...]
        o_refs[YS + d][:, SPAN:] = pair_of(k_ref, v_ref, head)


def swap_send_kernel(where_ref, kv_ref, o_ref):
    for j in range(YS):
        o_ref[j] = kv_ref[2 * j + where_ref[1]]


def gather_out_kernel(where_ref, *refs):
    y, z = where_ref[0], where_ref[1]
    for c in range(ZS):
        for d in range(YS):
            head = lax.rem(y + YS - d, YS) * ZS + jnp.bitwise_xor(z, c)
            columns(refs[-1], head * SPAN, SPAN)[...] = refs[c * YS + d][...]


def slots_kernel(target_ref, kv_ref, o_ref, slots, sem):
    pages = kv_ref.shape[1] // PAGE
    copies = []
    for t in (0, 1):
        part = slice(t * PAGE, (t + 1) * PAGE)
        slots[:, part, :] = jnp.zeros((slots.shape[0], PAGE, HEAD_DIM), slots.dtype)
        for b in range(kv_ref.shape[0]):
            for p in range(pages):
                rows = kv_ref[b, p * PAGE : (p + 1) * PAGE, t * HEAD_DIM : (t + 1) * HEAD_DIM]
                slots[target_ref[b * pages + p], part, :] = rows
        copies.append(pltpu.make_async_copy(slots.at[:, part, :], o_ref.at[:, part, :], sem.at[t]))
        copies[t].start()
    for copy in copies:
        copy.wait()


def caches_kernel(a_ref, k_ref, v_ref, parts, sem):
    count = parts.shape[0]
    slots = parts.shape[1]
    here = [pl.ds(i * slots, slots) for i in range(count)]
    into = [pltpu.make_async_copy(a_ref.at[here[i]], parts.at[i], sem.at[i]) for i in range(count)]
    for copy in into:
        copy.start()
    out = []
    for i in range(count):
        into[i].wait()
        for t, o_ref in enumerate((k_ref, v_ref)):
            part = parts.at[i, :, t * PAGE : (t + 1) * PAGE, :]
            out.append(pltpu.make_async_copy(part, o_ref.at[here[i]], sem.at[count + 2 * i + t]))
            out[-1].start()
    for copy in out:
        copy.wait()


def attend_kernel(rows, stored, where_ref, *refs):
    in_refs, o_refs, (q_all, kv_all, o_all, sem) = refs[: -YS - 4], refs[-YS - 4 : -4], refs[-4:]
    y, z = where_ref[0], where_ref[1]
    pairs = []
    for d in range(YS):
        j = lax.rem(y + YS - d, YS)
        part, more = in_refs[d], in_refs[YS]
        if stored:
            pairs += [(part, q_all.at[j])]
            pairs += [(more.at[2 * d + z], kv_all.at[0, d]), (more.at[2 * d + 1 - z], kv_all.at[1, d])]
        else:
            pairs += [(part.at[:, :SPAN], q_all.at[j]), (part.at[:, SPAN:], kv_all.at[0, j]), (more.at[d], kv_all.at[1, d])]
    move(pairs, sem)
    later = z == 1
    keep = lax.broadcasted_iota(jnp.int32, (rows, rows), 1) <= lax.broadcasted_iota(jnp.int32, (rows, rows), 0)
    dims = (((1,), (1,)), ((), ()))
    ones = jnp.ones((rows, HEAD_DIM), jnp.bfloat16)
    for i in range(YS):
        for h in range(GROUP):
            q = q_all[i, :, h * HEAD_DIM : (h + 1) * HEAD_DIM]
            parts = []
            for j in range(i + 1):
                for far in (0, 1):
                    s = lax.dot_general(q, kv_all[far, j, :, :HEAD_DIM], dims, preferred_element_type=jnp.float32)
                    if j == i:
                        s = jnp.where(later if far else keep, s, -jnp.inf)
                    parts.append((j, far, s))
            top = functools.reduce(jnp.maximum, [s for _, _, s in parts])
            top = jnp.max(top, axis=1, keepdims=True) * SCALE2
            total = jnp.zeros((rows, PAIR), jnp.float32)
            for j, far, s in parts:
                p = jnp.exp2(s * SCALE2 - top).astype(jnp.bfloat16)
                v = jnp.concatenate([kv_all[far, j, :, HEAD_DIM:], ones], axis=1)
                total += jnp.dot(p, v, preferred_element_type=jnp.float32)
            out = total[:, :HEAD_DIM] / total[:, HEAD_DIM:]
            o_all[i, :, h * HEAD_DIM : (h + 1) * HEAD_DIM] = out.astype(jnp.bfloat16)
    move([(o_all.at[lax.rem(y + d, YS)], o_refs[d]) for d in range(YS)], sem, len(pairs))


def across_z(x):
    return lax.ppermute(x, "zl", [(0, 1), (1, 0)])


def along_y(parts):
    got = [parts[0]] + [None] * (YS - 1)
    for d in (2, 1, 3):
        got[d] = lax.ppermute(parts[d], "y", [(i, (i + d) % YS) for i in range(YS)])
    return got


def local(queries, keys, values, page_owner):
    count = lax.axis_size(GRP)
    rows = queries.shape[1]
    bf16 = lambda *shape: jax.ShapeDtypeStruct(shape, jnp.bfloat16)
    where = jnp.stack([lax.axis_index("y"), lax.axis_index("zl")]).astype(jnp.int32)

    k, v, q = keys[0], values[0], queries[0]
    kv_send = call(
        kv_send_kernel,
        bf16(KV_HEADS, rows, PAIR),
        (k, v),
        3,
        scratch=[
            pltpu.VMEM(k.shape, jnp.bfloat16),
            pltpu.VMEM(v.shape, jnp.bfloat16),
            pltpu.VMEM((KV_HEADS, rows, PAIR), jnp.bfloat16),
        ],
        space=pl.ANY,
        vmem=60,
        name="kv_send",
        moved=2 * 2**20,
    )
    owners = page_owner[0, :, 0]
    onehot = (owners[:, None] == jnp.arange(count)[None, :]).astype(jnp.int32)
    rank = jnp.sum(onehot * (jnp.cumsum(onehot, axis=0) - 1), axis=1)
    target = owners * MOST + rank
    kv_send, q, k, v = lax.optimization_barrier((kv_send, q, k, v))
    kv = lax.all_to_all(kv_send, SP, split_axis=0, concat_axis=0, tiled=True)
    *q_parts, r0, r1, r2, r3 = call(
        q_send_kernel,
        [bf16(rows, SPAN)] * YS + [bf16(rows, SPAN + PAIR)] * YS,
        (where, q, k, v),
        name="q_send",
        moved=5 * 2**20,
    )
    rest = [r0, r1, r2, r3]
    q_got = along_y(q_parts)
    swapped = across_z(
        call(swap_send_kernel, bf16(YS, rows, PAIR), (where, kv), name="swap_send", moved=2**20)
    )

    slots = call(
        slots_kernel,
        bf16(count * MOST, 2 * PAGE, HEAD_DIM),
        (target, kv),
        2,
        scratch=[pltpu.VMEM((count * MOST, 2 * PAGE, HEAD_DIM), jnp.bfloat16)],
        out_space=pl.ANY,
        name="slots",
        moved=3 * 2**20,
    )
    slots, rest = lax.optimization_barrier((slots, rest))
    kv, swapped = lax.optimization_barrier((kv, swapped))
    arrived = lax.all_to_all(slots, GRP, split_axis=0, concat_axis=0, tiled=True)
    key_cache, value_cache = call(
        caches_kernel,
        [bf16(count * MOST, PAGE, HEAD_DIM)] * 2,
        (arrived,),
        12,
        scratch=[pltpu.VMEM((4, count * MOST // 4, 2 * PAGE, HEAD_DIM), jnp.bfloat16)],
        space=pl.ANY,
        name="caches",
        moved=4 * 2**20,
    )

    rest_got = along_y(rest)
    got = []
    for stored, ins in ((True, (*q_got, kv)), (False, (*rest_got, swapped))):
        o_parts = call(
            functools.partial(attend_kernel, rows, stored),
            [bf16(rows, SPAN)] * YS,
            (where, *ins),
            4 * YS,
            scratch=[
                pltpu.VMEM((YS, rows, SPAN), jnp.bfloat16),
                pltpu.VMEM((ZS, YS, rows, PAIR), jnp.bfloat16),
                pltpu.VMEM((YS, rows, SPAN), jnp.bfloat16),
            ],
            space=pl.ANY,
            vmem=20,
            name="attend",
            flops=(200 if stored else 10) * 10**9,
            moved=4 * 2**20,
            exps=5 * 10**6,
        )
        got += along_y(o_parts)
    attention = call(
        gather_out_kernel,
        bf16(rows, Q_HEADS * HEAD_DIM),
        (where, *got),
        name="gather_out",
        moved=4 * 2**20,
    )
    return attention[None], key_cache, value_cache


def solution(mesh):
    parts = Mesh(mesh.devices.reshape(4, 4, 2, YS, ZS), GRP + SP)
    return jax.shard_map(
        local,
        mesh=parts,
        in_specs=(P(GRP, SP, None), P(GRP, SP, None), P(GRP, SP, None), P(GRP, None, None)),
        out_specs=(P(GRP, SP, None), P(GRP, None, SP), P(GRP, None, SP)),
        check_vma=False,
    )
```

```python
import functools

import jax
import jax.numpy as jnp
from jax import lax
from jax.experimental import pallas as pl
from jax.experimental.pallas import tpu as pltpu
from jax.sharding import Mesh, PartitionSpec as P

Q_HEADS = 32
KV_HEADS = 8
HEAD_DIM = 128
GROUP = Q_HEADS // KV_HEADS
SPAN = GROUP * HEAD_DIM
PAIR = 2 * HEAD_DIM
PAGE = 16
MOST = 8
LOG2E = 1.4426950408889634
SCALE2 = HEAD_DIM**-0.5 * LOG2E
GRP = ("zh", "x", "core")
SP = ("y", "zl")
YS = 4
ZS = 2
FIRST = (0, 1, 2, 3)
SHIFTS = (0, 2, 1, 3)


def call(kernel, outs, ins, copies=1, scratch=(), space=pltpu.VMEM, out_space=None, vmem=12, name=None, flops=0, moved=0, exps=0):
    out_space = out_space or space
    return pl.pallas_call(
        kernel,
        out_shape=outs,
        in_specs=[pl.BlockSpec(memory_space=pltpu.SMEM if x.dtype == jnp.int32 else space) for x in ins],
        out_specs=jax.tree.map(lambda _: pl.BlockSpec(memory_space=out_space), outs),
        scratch_shapes=[*scratch, *([pltpu.SemaphoreType.DMA((copies,))] if out_space == pl.ANY else [])],
        compiler_params=pltpu.CompilerParams(vmem_limit_bytes=vmem * 2**20),
        cost_estimate=pl.CostEstimate(flops=flops, bytes_accessed=moved, transcendentals=exps),
        name=name,
    )(*ins)


def move(pairs, sem, first=0):
    copies = [pltpu.make_async_copy(src, dst, sem.at[first + i]) for i, (src, dst) in enumerate(pairs)]
    for copy in copies:
        copy.start()
    for copy in copies:
        copy.wait()


def columns(ref, start, width):
    return ref.at[:, pl.ds(pl.multiple_of(start, width), width)]


def pair_of(k_ref, v_ref, head):
    return jnp.concatenate([columns(r, head * HEAD_DIM, HEAD_DIM)[...] for r in (k_ref, v_ref)], axis=1)


def kv_send_kernel(k_ref, v_ref, o_ref, k, v, out, sem):
    rows = k.shape[0] // 2
    halves = [slice(i * rows, (i + 1) * rows) for i in (0, 1)]
    into = [
        pltpu.make_async_copy(src.at[half], dst.at[half], sem.at[2 * i + t])
        for i, half in enumerate(halves)
        for t, (src, dst) in enumerate(((k_ref, k), (v_ref, v)))
    ]
    for copy in into:
        copy.start()
    away = []
    for i, half in enumerate(halves):
        into[2 * i].wait()
        into[2 * i + 1].wait()
        for h in range(KV_HEADS):
            cols = slice(h * HEAD_DIM, (h + 1) * HEAD_DIM)
            out[h, half, :HEAD_DIM] = k[half, cols]
            out[h, half, HEAD_DIM:] = v[half, cols]
        away.append(pltpu.make_async_copy(out.at[:, half], o_ref.at[:, half], sem.at[4 + i]))
        away[i].start()
    for copy in away:
        copy.wait()


def q_send_kernel(where_ref, q_ref, k_ref, v_ref, *o_refs):
    y, z = where_ref[0], where_ref[1]
    for n, d in enumerate(FIRST):
        head = lax.rem(y + d, YS) * ZS + z
        o_refs[n][...] = columns(q_ref, head * SPAN, SPAN)[...]
    for n, d in enumerate(SHIFTS):
        head = lax.rem(y + d, YS) * ZS + 1 - z
        o_refs[YS + n][:, :SPAN] = columns(q_ref, head * SPAN, SPAN)[...]
        o_refs[YS + n][:, SPAN:] = pair_of(k_ref, v_ref, head)


def swap_send_kernel(where_ref, kv_ref, o_ref):
    for j in range(YS):
        o_ref[j] = kv_ref[2 * j + where_ref[1]]


def gather_out_kernel(where_ref, *refs):
    y, z = where_ref[0], where_ref[1]
    for c in range(ZS):
        for n, d in enumerate(SHIFTS):
            head = lax.rem(y + YS - d, YS) * ZS + jnp.bitwise_xor(z, c)
            columns(refs[-1], head * SPAN, SPAN)[...] = refs[c * YS + n][...]


def slots_kernel(target_ref, kv_ref, o_ref, slots, sem):
    pages = kv_ref.shape[1] // PAGE
    copies = []
    for t in (0, 1):
        part = slice(t * PAGE, (t + 1) * PAGE)
        slots[:, part, :] = jnp.zeros((slots.shape[0], PAGE, HEAD_DIM), slots.dtype)
        for b in range(kv_ref.shape[0]):
            for p in range(pages):
                rows = kv_ref[b, p * PAGE : (p + 1) * PAGE, t * HEAD_DIM : (t + 1) * HEAD_DIM]
                slots[target_ref[b * pages + p], part, :] = rows
        copies.append(pltpu.make_async_copy(slots.at[:, part, :], o_ref.at[:, part, :], sem.at[t]))
        copies[t].start()
    for copy in copies:
        copy.wait()


def caches_kernel(a_ref, k_ref, v_ref, parts, sem):
    count = parts.shape[0]
    slots = parts.shape[1]
    here = [pl.ds(i * slots, slots) for i in range(count)]
    into = [pltpu.make_async_copy(a_ref.at[here[i]], parts.at[i], sem.at[i]) for i in range(count)]
    for copy in into:
        copy.start()
    out = []
    for i in range(count):
        into[i].wait()
        for t, o_ref in enumerate((k_ref, v_ref)):
            part = parts.at[i, :, t * PAGE : (t + 1) * PAGE, :]
            out.append(pltpu.make_async_copy(part, o_ref.at[here[i]], sem.at[count + 2 * i + t]))
            out[-1].start()
    for copy in out:
        copy.wait()


def attend_kernel(rows, stored, where_ref, *refs):
    in_refs, o_refs, (q_all, kv_all, o_all, sem) = refs[: -YS - 4], refs[-YS - 4 : -4], refs[-4:]
    y, z = where_ref[0], where_ref[1]
    pairs = []
    for n, d in enumerate(FIRST if stored else SHIFTS):
        j = lax.rem(y + YS - d, YS)
        part, more = in_refs[n], in_refs[YS]
        if stored:
            pairs += [(part, q_all.at[j])]
            pairs += [(more.at[2 * n + z], kv_all.at[0, n]), (more.at[2 * n + 1 - z], kv_all.at[1, n])]
        else:
            pairs += [(part.at[:, :SPAN], q_all.at[j]), (part.at[:, SPAN:], kv_all.at[0, j]), (more.at[n], kv_all.at[1, n])]
    move(pairs, sem)
    later = z == 1
    keep = lax.broadcasted_iota(jnp.int32, (rows, rows), 1) <= lax.broadcasted_iota(jnp.int32, (rows, rows), 0)
    dims = (((1,), (1,)), ((), ()))
    ones = jnp.ones((rows, HEAD_DIM), jnp.bfloat16)
    for i in range(YS):
        for h in range(GROUP):
            q = q_all[i, :, h * HEAD_DIM : (h + 1) * HEAD_DIM]
            parts = []
            for j in range(i + 1):
                for far in (0, 1):
                    s = lax.dot_general(q, kv_all[far, j, :, :HEAD_DIM], dims, preferred_element_type=jnp.float32)
                    if j == i:
                        s = jnp.where(later if far else keep, s, -jnp.inf)
                    parts.append((j, far, s))
            top = functools.reduce(jnp.maximum, [s for _, _, s in parts])
            top = jnp.max(top, axis=1, keepdims=True) * SCALE2
            total = jnp.zeros((rows, PAIR), jnp.float32)
            for j, far, s in parts:
                p = jnp.exp2(s * SCALE2 - top).astype(jnp.bfloat16)
                v = jnp.concatenate([kv_all[far, j, :, HEAD_DIM:], ones], axis=1)
                total += jnp.dot(p, v, preferred_element_type=jnp.float32)
            out = total[:, :HEAD_DIM] / total[:, HEAD_DIM:]
            o_all[i, :, h * HEAD_DIM : (h + 1) * HEAD_DIM] = out.astype(jnp.bfloat16)
    move([(o_all.at[lax.rem(y + d, YS)], o_refs[n]) for n, d in enumerate(SHIFTS)], sem, len(pairs))


def across_z(x):
    return lax.ppermute(x, "zl", [(0, 1), (1, 0)])


def along_y(parts, shifts=SHIFTS):
    return [
        lax.ppermute(part, "y", [(i, (i + d) % YS) for i in range(YS)]) if d else part
        for part, d in zip(parts, shifts, strict=True)
    ]


def local(queries, keys, values, page_owner):
    count = lax.axis_size(GRP)
    rows = queries.shape[1]
    bf16 = lambda *shape: jax.ShapeDtypeStruct(shape, jnp.bfloat16)
    where = jnp.stack([lax.axis_index("y"), lax.axis_index("zl")]).astype(jnp.int32)

    k, v, q = keys[0], values[0], queries[0]
    kv_send = call(
        kv_send_kernel,
        bf16(KV_HEADS, rows, PAIR),
        (k, v),
        6,
        scratch=[
            pltpu.VMEM(k.shape, jnp.bfloat16),
            pltpu.VMEM(v.shape, jnp.bfloat16),
            pltpu.VMEM((KV_HEADS, rows, PAIR), jnp.bfloat16),
        ],
        space=pl.ANY,
        vmem=60,
        name="kv_send",
        moved=2 * 2**20,
    )
    owners = page_owner[0, :, 0]
    onehot = (owners[:, None] == jnp.arange(count)[None, :]).astype(jnp.int32)
    rank = jnp.sum(onehot * (jnp.cumsum(onehot, axis=0) - 1), axis=1)
    target = owners * MOST + rank
    kv_send, q, k, v = lax.optimization_barrier((kv_send, q, k, v))
    kv = lax.all_to_all(kv_send, SP, split_axis=0, concat_axis=0, tiled=True)
    *q_parts, r0, r1, r2, r3 = call(
        q_send_kernel,
        [bf16(rows, SPAN)] * YS + [bf16(rows, SPAN + PAIR)] * YS,
        (where, q, k, v),
        name="q_send",
        moved=5 * 2**20,
    )
    rest = [r0, r1, r2, r3]
    q_got = along_y(q_parts, FIRST)
    swapped = across_z(
        call(swap_send_kernel, bf16(YS, rows, PAIR), (where, kv), name="swap_send", moved=2**20)
    )

    slots = call(
        slots_kernel,
        bf16(count * MOST, 2 * PAGE, HEAD_DIM),
        (target, kv),
        2,
        scratch=[pltpu.VMEM((count * MOST, 2 * PAGE, HEAD_DIM), jnp.bfloat16)],
        out_space=pl.ANY,
        name="slots",
        moved=3 * 2**20,
    )
    kv, swapped, rest = lax.optimization_barrier((kv, swapped, rest))
    arrived = lax.all_to_all(slots, GRP, split_axis=0, concat_axis=0, tiled=True)
    key_cache, value_cache = call(
        caches_kernel,
        [bf16(count * MOST, PAGE, HEAD_DIM)] * 2,
        (arrived,),
        12,
        scratch=[pltpu.VMEM((4, count * MOST // 4, 2 * PAGE, HEAD_DIM), jnp.bfloat16)],
        space=pl.ANY,
        name="caches",
        moved=4 * 2**20,
    )

    rest_got = along_y(rest)
    got = []
    for stored, ins in ((True, (*q_got, kv)), (False, (*rest_got, swapped))):
        o_parts = call(
            functools.partial(attend_kernel, rows, stored),
            [bf16(rows, SPAN)] * YS,
            (where, *ins),
            4 * YS,
            scratch=[
                pltpu.VMEM((YS, rows, SPAN), jnp.bfloat16),
                pltpu.VMEM((ZS, YS, rows, PAIR), jnp.bfloat16),
                pltpu.VMEM((YS, rows, SPAN), jnp.bfloat16),
            ],
            space=pl.ANY,
            vmem=20,
            name="attend",
            flops=(200 if stored else 10) * 10**9,
            moved=4 * 2**20,
            exps=5 * 10**6,
        )
        got += along_y(o_parts)
    attention = call(
        gather_out_kernel,
        bf16(rows, Q_HEADS * HEAD_DIM),
        (where, *got),
        name="gather_out",
        moved=4 * 2**20,
    )
    return attention[None], key_cache, value_cache


def solution(mesh):
    parts = Mesh(mesh.devices.reshape(4, 4, 2, YS, ZS), GRP + SP)
    return jax.shard_map(
        local,
        mesh=parts,
        in_specs=(P(GRP, SP, None), P(GRP, SP, None), P(GRP, SP, None), P(GRP, None, None)),
        out_specs=(P(GRP, SP, None), P(GRP, None, SP), P(GRP, None, SP)),
        check_vma=False,
    )
```
